32 devices in a mesh: row: 8 (over y, x, core), col: 4 (over z).
Axes of the slice: x: 2, y: 2, z: 4, core: 2. Of those that a mesh axis runs over, the one named last changes fastest.
Arguments:
- amplitudes: bfloat16 [6144, 6144], P('row', 'col'), may hold values from -6 to 6
- integrals: bfloat16 [6144, 6144], P('row', 'col'), may hold values from -0.078125 to 0.078125
- dressing: bfloat16 [6144, 3072], P(None, 'col'), may hold values from -0.078125 to 0.078125
Outputs:
- first_cycle: float32 [6144, 6144], P('row', 'col')
- second_cycle: float32 [6144, 3072], P('row', 'col')
The draws below stay inside these ranges and needn't reach their ends.
All inputs are finite; a program needn't handle non-finite values.
Results may differ from the reference program's by a relative error of at most 0.0029.
Values may be sent and summed in bfloat16 or wider, within the bound.
A program may use at most 128 MiB of HBM per device.

```python
import jax
import jax.numpy as jnp

NV = 3072
OCC = 2
SLICE = 192
N_ROW = 8
N_COL = 4


def level_of(rng, shape, shards, smallest, high):
    level = 1.0
    for position, parts in shards:
        draws = jax.random.uniform(jax.random.fold_in(jax.random.fold_in(rng, 6), position), (parts,), jnp.float32, smallest / len(shards), high / len(shards))
        level = level * jnp.repeat(jnp.exp(draws), shape[position] // parts).reshape((-1,) + (1,) * (len(shape) - 1 - position))
    return level


def noise(stream_key, extent, spread, reach, split=(), dtype=jnp.bfloat16):
    gain = level_of(stream_key, extent, split, -0.22, 0.18) if split else 1.0
    values = jax.random.normal(stream_key, extent, jnp.float32) * spread * gain
    return jnp.minimum(jnp.maximum(values, -reach), reach).astype(dtype)


def setup_inputs(seed: int = 0) -> dict:
    splits = jax.random.split(jax.random.key(seed), 4)
    return {
        "amplitudes": noise(splits[0], (OCC * NV, OCC * NV), 1.0, 6.0, ((0, 8), (1, 4))),
        "integrals": noise(splits[1], (OCC * NV, OCC * NV), (OCC * NV) ** -0.5, 0.078125, ((0, 8), (1, 4))),
        "dressing": noise(splits[2], (OCC * NV, NV), (OCC * NV) ** -0.5, 0.078125, ((1, 4),)),
    }


def reference(amplitudes, integrals, dressing):
    first_cycle = jnp.dot(amplitudes, integrals, preferred_element_type=jnp.float32)
    rounded = first_cycle.astype(jnp.bfloat16)
    cycle = jnp.dot(rounded.T, dressing, preferred_element_type=jnp.float32)
    second_cycle = cycle.reshape(N_COL, N_ROW, SLICE, NV).transpose(1, 0, 2, 3).reshape(OCC * NV, NV)
    return first_cycle, second_cycle
```

```python
import functools

import jax
import jax.numpy as jnp
from jax import lax
from jax.experimental import pallas as pl
from jax.experimental.pallas import tpu as pltpu
from jax.sharding import PartitionSpec as P

MESH = pl.DeviceIdType.MESH
F32 = jnp.float32


def tile_of(size, largest):
    return max(t for t in range(128, largest + 1, 128) if size % t == 0)


def kernel(
    n_row, n_col, part,
    a_ref, b_ref, d_ref, c_ref, out_ref,
    abuf, bbuf, dbuf, acc, turned, mine, chipsum, others,
    a_send, a_recv, d_send, d_recv, b_send, b_recv, s_send, s_recv,
    x_send, x_recv, r_send, r_recv, o_send, o_recv, local,
):
    n_chip = n_row // 2
    r, q = lax.axis_index("row"), lax.axis_index("col")
    core, chip = lax.rem(r, 2), lax.div(r, 2)
    sibling = r + 1 - 2 * core
    a_rows, depth = a_ref.shape
    b_rows, width = b_ref.shape
    d_cols = d_ref.shape[1]

    def peer(dist):
        return lax.rem(chip + dist, n_chip) * 2 + core

    def order(i):
        room = jnp.minimum(q, n_col - 1 - q)
        half = lax.div(i + 1, 2)
        near = jnp.where(lax.rem(i, 2) == 1, q - half, q + half)
        far = jnp.where(q <= n_col - 1 - q, i, n_col - 1 - i)
        return jnp.where(i <= 2 * room, near, far)

    def remote(src, dst, send, recv, where):
        return pltpu.make_async_remote_copy(
            src_ref=src, dst_ref=dst, send_sem=send, recv_sem=recv, device_id=where, device_id_type=MESH
        )

    barrier = pltpu.get_barrier_semaphore()
    partners = [{"row": peer(k)} for k in range(1, n_chip)] + [{"row": sibling}]
    partners += [{"col": lax.rem(q + k, n_col)} for k in range(1, n_col)]
    for where in partners:
        pl.semaphore_signal(barrier, inc=1, device_id=where, device_id_type=MESH)
    pl.semaphore_wait(barrier, len(partners))

    def b_slot(owner):
        return bbuf.at[pl.ds(pl.multiple_of(owner * b_rows, b_rows), b_rows), :]

    def b_copy(k):
        return remote(b_ref, b_slot(r), b_send.at[k], b_recv.at[k], {"row": peer(k)})

    def b_arrival(k):
        slot = b_slot(peer(n_chip - k))
        return remote(slot, slot, b_send.at[k], b_recv.at[k], {"row": peer(k)})

    def s_copy(k):
        slot = b_slot(peer(n_chip - k))
        src = b_ref if k == 0 else slot
        return remote(src, slot, s_send.at[k], s_recv.at[k], {"row": sibling})

    def s_arrival(k):
        slot = b_slot(lax.rem(chip + n_chip - k, n_chip) * 2 + 1 - core)
        return remote(slot, slot, s_send.at[k], s_recv.at[k], {"row": sibling})

    own_d = d_ref.at[pl.ds(pl.multiple_of(r * a_rows, a_rows), a_rows), :]

    def line_copy(own, buf, send, recv, z, side, is_own):
        src = own if is_own else buf.at[z]
        return remote(src, buf.at[z], send.at[z, side], recv.at[z], {"col": q - 1 + 2 * side})

    def line_start(own, buf, send, recv):
        @pl.when(q > 0)
        def _():
            line_copy(own, buf, send, recv, q, 0, True).start()

        @pl.when(q < n_col - 1)
        def _():
            line_copy(own, buf, send, recv, q, 1, True).start()

    def line_forward(own, buf, send, recv, z):
        side = jnp.where(z < q, 0, 1)
        line_copy(own, buf, send, recv, z, side, False).wait_recv()

        @pl.when((z < q) & (q < n_col - 1))
        def _():
            line_copy(own, buf, send, recv, z, 1, False).start()

        @pl.when((z > q) & (q > 0))
        def _():
            line_copy(own, buf, send, recv, z, 0, False).start()

    def line_drain(own, buf, send, recv):
        @pl.loop(0, n_col)
        def _(z):
            @pl.when((z <= q) & (q < n_col - 1))
            def _():
                line_copy(own, buf, send, recv, z, 1, False).wait_send()

            @pl.when((z >= q) & (q > 0))
            def _():
                line_copy(own, buf, send, recv, z, 0, False).wait_send()

    a_line = (a_ref, abuf, a_send, a_recv)
    d_line = (own_d, dbuf, d_send, d_recv)

    line_start(*a_line)
    for k in range(1, n_chip):
        b_copy(k).start()
    s_copy(0).start()
    loads = [
        pltpu.make_async_copy(a_ref, abuf.at[q], local.at[0]),
        pltpu.make_async_copy(b_ref, b_slot(r), local.at[1]),
        pltpu.make_async_copy(own_d, dbuf.at[q], local.at[2]),
    ]
    for load in loads:
        load.start()
    for load in loads:
        load.wait()

    middle = n_col // 2 + 1

    @pl.loop(1, middle)
    def _(i):
        line_forward(*a_line, order(i))

    line_start(*d_line)
    for k in range(1, n_chip):
        b_arrival(k).wait_recv()
        s_copy(k).start()

    def multiply(z):
        tile = tile_of(width, 256)

        @pl.loop(0, width // tile)
        def _(j):
            cols = pl.ds(pl.multiple_of(j * tile, tile), tile)
            rows = pl.ds(pl.multiple_of(z * depth, depth), depth)
            acc[:, cols] += jnp.dot(abuf[z], bbuf[rows, cols], preferred_element_type=F32)

    acc[...] = jnp.zeros_like(acc)
    for k in range(n_chip):
        s_arrival(k).wait_recv()

    @pl.loop(0, n_col)
    def _(i):
        @pl.when(i >= middle)
        def _():
            line_forward(*a_line, order(i))

        multiply(order(i))

    first_out = pltpu.make_async_copy(acc, c_ref, local.at[3])
    first_out.start()
    turn = tile_of(width, 256)

    @pl.loop(0, width // turn)
    def _(j):
        at = pl.ds(pl.multiple_of(j * turn, turn), turn)
        turned[at, :] = acc[:, at].T.astype(turned.dtype)

    def x_copy(z):
        return remote(mine.at[1 - core], chipsum.at[z], x_send.at[z], x_recv.at[z], {"row": sibling})

    def r_copy(z, k):
        target = lax.rem(chip + k, n_chip)
        return remote(
            chipsum.at[z, target], others.at[z, k - 1], r_send.at[z, k], r_recv.at[z, k], {"row": peer(k)}
        )

    def o_copy(z, sem):
        place = out_ref.at[pl.ds(pl.multiple_of(q * part, part), part), :]
        return remote(chipsum.at[z, chip], place, o_send.at[z], o_recv.at[sem], {"col": z})

    def o_arrival(z):
        place = out_ref.at[pl.ds(pl.multiple_of(z * part, part), part), :]
        return remote(place, place, o_send.at[z], o_recv.at[z], {"col": z})

    def o_own():
        place = out_ref.at[pl.ds(pl.multiple_of(q * part, part), part), :]
        return pltpu.make_async_copy(chipsum.at[q, chip], place, local.at[4])

    def finish(z):
        for k in range(1, n_chip):
            r_copy(z, k).wait_recv()
        total = chipsum[z, chip]
        for k in range(1, n_chip):
            total += others[z, k - 1]
        chipsum[z, chip] = total

        @pl.when(z == q)
        def _():
            o_own().start()

        @pl.when(z != q)
        def _():
            o_copy(z, q).start()

    @pl.loop(0, n_col)
    def _(i):
        z = order(i)

        @pl.when(i > 0)
        def _():
            line_forward(*d_line, z)
            x_copy(order(i - 1)).wait_send()

        tile = tile_of(d_cols, 256)

        @pl.loop(0, d_cols // tile)
        def _(j):
            cols = pl.ds(pl.multiple_of(j * tile, tile), tile)
            product = jnp.dot(turned[...], dbuf[z, :, cols], preferred_element_type=F32)
            for owner in range(n_row):
                mine[owner % 2, owner // 2, :, cols] = product[owner * part : (owner + 1) * part]

        x_copy(z).start()

        @pl.when(i > 0)
        def _():
            finish(order(i - 1))

        x_copy(z).wait_recv()
        for k in range(n_chip):
            chipsum[z, k] += mine[core, k]
        for k in range(1, n_chip):
            r_copy(z, k).start()

    last = order(jnp.int32(n_col - 1))
    finish(last)

    x_copy(last).wait_send()
    line_drain(*a_line)
    line_drain(*d_line)
    for k in range(1, n_chip):
        b_copy(k).wait_send()
    for k in range(n_chip):
        s_copy(k).wait_send()

    @pl.loop(0, n_col)
    def _(z):
        for k in range(1, n_chip):
            r_copy(z, k).wait_send()

        @pl.when(z != q)
        def _():
            o_copy(z, q).wait_send()
            o_arrival(z).wait_recv()

    o_own().wait()
    first_out.wait()


def per_device(n_row, n_col, amplitudes, integrals, dressing):
    rows, depth = amplitudes.shape
    width, d_cols = integrals.shape[1], dressing.shape[1]
    part, n_chip = width // n_row, n_row // 2
    bf16 = amplitudes.dtype
    dma = pltpu.SemaphoreType.DMA
    anywhere = pl.BlockSpec(memory_space=pl.ANY)
    total = depth * n_col
    return tuple(
        pl.pallas_call(
            functools.partial(kernel, n_row, n_col, part),
            out_shape=[
                jax.ShapeDtypeStruct((rows, width), F32),
                jax.ShapeDtypeStruct((part * n_col, d_cols), F32),
            ],
            in_specs=[anywhere] * 3,
            out_specs=[anywhere] * 2,
            scratch_shapes=[
                pltpu.VMEM((n_col, rows, depth), bf16),
                pltpu.VMEM((total, width), bf16),
                pltpu.VMEM((n_col, rows, d_cols), bf16),
                pltpu.VMEM((rows, width), F32),
                pltpu.VMEM((width, rows), bf16),
                pltpu.VMEM((2, n_chip, part, d_cols), F32),
                pltpu.VMEM((n_col, n_chip, part, d_cols), F32),
                pltpu.VMEM((n_col, n_chip - 1, part, d_cols), F32),
                dma((n_col, 2)), dma((n_col,)), dma((n_col, 2)), dma((n_col,)),
                dma((n_chip,)), dma((n_chip,)), dma((n_chip,)), dma((n_chip,)),
                dma((n_col,)), dma((n_col,)),
                dma((n_col, n_chip)), dma((n_col, n_chip)),
                dma((n_col,)), dma((n_col,)),
                dma((5,)),
            ],
            compiler_params=pltpu.CompilerParams(
                collective_id=0, has_side_effects=True, vmem_limit_bytes=62 * 2**20
            ),
            cost_estimate=pl.CostEstimate(
                flops=2 * rows * width * (total + d_cols * n_col),
                bytes_accessed=2 * total * (rows + width),
                transcendentals=0,
            ),
        )(amplitudes, integrals, dressing)
    )


def solution(mesh):
    placed = (P("row", "col"), P("row", "col"), P(None, "col"))
    return jax.shard_map(
        functools.partial(per_device, mesh.shape["row"], mesh.shape["col"]),
        mesh=mesh,
        in_specs=placed,
        out_specs=(P("row", "col"), P("row", "col")),
        check_vma=False,
    )
```

```python
import functools

import jax
import jax.numpy as jnp
from jax import lax
from jax.experimental import pallas as pl
from jax.experimental.pallas import tpu as pltpu
from jax.sharding import PartitionSpec as P

MESH = pl.DeviceIdType.MESH
F32 = jnp.float32


def tile_of(size, largest):
    return max(t for t in range(128, largest + 1, 128) if size % t == 0)


def kernel(
    n_row, n_col, part,
    a_ref, b_ref, d_ref, c_ref, out_ref,
    abuf, bbuf, dbuf, acc, turned, mine, chipsum, sent, others, landed,
    a_send, a_recv, d_send, d_recv, b_send, b_recv, s_send, s_recv,
    x_send, x_recv, r_send, r_recv, o_send, o_recv, stored, local,
):
    n_chip = n_row // 2
    r, q = lax.axis_index("row"), lax.axis_index("col")
    core, chip = lax.rem(r, 2), lax.div(r, 2)
    sibling = r + 1 - 2 * core
    a_rows, depth = a_ref.shape
    b_rows, width = b_ref.shape
    d_cols = d_ref.shape[1]

    def peer(dist):
        return lax.rem(chip + dist, n_chip) * 2 + core

    def order(i):
        room = jnp.minimum(q, n_col - 1 - q)
        half = lax.div(i + 1, 2)
        near = jnp.where(lax.rem(i, 2) == 1, q - half, q + half)
        far = jnp.where(q <= n_col - 1 - q, i, n_col - 1 - i)
        return jnp.where(i <= 2 * room, near, far)

    def remote(src, dst, send, recv, where):
        return pltpu.make_async_remote_copy(
            src_ref=src, dst_ref=dst, send_sem=send, recv_sem=recv, device_id=where, device_id_type=MESH
        )

    barrier = pltpu.get_barrier_semaphore()
    partners = [{"row": peer(k)} for k in range(1, n_chip)] + [{"row": sibling}]
    partners += [{"col": lax.rem(q + k, n_col)} for k in range(1, n_col)]
    for where in partners:
        pl.semaphore_signal(barrier, inc=1, device_id=where, device_id_type=MESH)
    pl.semaphore_wait(barrier, len(partners))

    def b_slot(owner):
        return bbuf.at[pl.ds(pl.multiple_of(owner * b_rows, b_rows), b_rows), :]

    def b_copy(k):
        return remote(b_ref, b_slot(r), b_send.at[k], b_recv.at[k], {"row": peer(k)})

    def b_arrival(k):
        slot = b_slot(peer(n_chip - k))
        return remote(slot, slot, b_send.at[k], b_recv.at[k], {"row": peer(k)})

    def s_copy(k):
        slot = b_slot(peer(n_chip - k))
        src = b_ref if k == 0 else slot
        return remote(src, slot, s_send.at[k], s_recv.at[k], {"row": sibling})

    def s_arrival(k):
        slot = b_slot(lax.rem(chip + n_chip - k, n_chip) * 2 + 1 - core)
        return remote(slot, slot, s_send.at[k], s_recv.at[k], {"row": sibling})

    own_d = d_ref.at[pl.ds(pl.multiple_of(r * a_rows, a_rows), a_rows), :]

    def line_copy(own, buf, send, recv, z, side, is_own):
        src = own if is_own else buf.at[z]
        return remote(src, buf.at[z], send.at[z, side], recv.at[z], {"col": q - 1 + 2 * side})

    def line_start(own, buf, send, recv):
        @pl.when(q > 0)
        def _():
            line_copy(own, buf, send, recv, q, 0, True).start()

        @pl.when(q < n_col - 1)
        def _():
            line_copy(own, buf, send, recv, q, 1, True).start()

    def line_forward(own, buf, send, recv, z):
        side = jnp.where(z < q, 0, 1)
        line_copy(own, buf, send, recv, z, side, False).wait_recv()

        @pl.when((z < q) & (q < n_col - 1))
        def _():
            line_copy(own, buf, send, recv, z, 1, False).start()

        @pl.when((z > q) & (q > 0))
        def _():
            line_copy(own, buf, send, recv, z, 0, False).start()

    def line_drain(own, buf, send, recv):
        @pl.loop(0, n_col)
        def _(z):
            @pl.when((z <= q) & (q < n_col - 1))
            def _():
                line_copy(own, buf, send, recv, z, 1, False).wait_send()

            @pl.when((z >= q) & (q > 0))
            def _():
                line_copy(own, buf, send, recv, z, 0, False).wait_send()

    a_line = (a_ref, abuf, a_send, a_recv)
    d_line = (own_d, dbuf, d_send, d_recv)

    line_start(*a_line)
    for k in range(1, n_chip):
        b_copy(k).start()
    s_copy(0).start()
    loads = [
        pltpu.make_async_copy(a_ref, abuf.at[q], local.at[0]),
        pltpu.make_async_copy(b_ref, b_slot(r), local.at[1]),
        pltpu.make_async_copy(own_d, dbuf.at[q], local.at[2]),
    ]
    for load in loads:
        load.start()
    for load in loads:
        load.wait()

    at_end = (q == 0) | (q == n_col - 1)
    early = jnp.where(at_end, n_col // 2 + 1, n_col)

    @pl.loop(1, early)
    def _(i):
        line_forward(*a_line, order(i))

    @pl.when(at_end)
    def _():
        line_start(*d_line)

    for k in range(1, n_chip):
        b_arrival(k).wait_recv()
        s_copy(k).start()

    def multiply(z):
        tile = tile_of(width, 256)

        @pl.loop(0, width // tile)
        def _(j):
            cols = pl.ds(pl.multiple_of(j * tile, tile), tile)
            rows = pl.ds(pl.multiple_of(z * depth, depth), depth)
            acc[:, cols] += jnp.dot(abuf[z], bbuf[rows, cols], preferred_element_type=F32)

    acc[...] = jnp.zeros_like(acc)
    for k in range(n_chip):
        s_arrival(k).wait_recv()

    @pl.loop(0, n_col)
    def _(i):
        @pl.when(i >= early)
        def _():
            line_forward(*a_line, order(i))

        multiply(order(i))

    @pl.when(jnp.logical_not(at_end))
    def _():
        line_start(*d_line)

    first_out = pltpu.make_async_copy(acc, c_ref, local.at[3])
    first_out.start()
    turn = tile_of(width, 256)

    @pl.loop(0, width // turn)
    def _(j):
        at = pl.ds(pl.multiple_of(j * turn, turn), turn)
        turned[at, :] = acc[:, at].T.astype(turned.dtype)

    def x_copy(z):
        return remote(mine.at[1 - core], chipsum.at[z], x_send.at[z], x_recv.at[z], {"row": sibling})

    def r_copy(z, k):
        return remote(
            sent.at[z, k - 1], others.at[z, k - 1], r_send.at[z, k], r_recv.at[z, k], {"row": peer(k)}
        )

    def o_copy(z):
        return remote(others.at[z, 0], landed.at[q], o_send.at[z], o_recv.at[q], {"col": z})

    def o_arrival(z):
        return remote(landed.at[z], landed.at[z], o_send.at[z], o_recv.at[z], {"col": z})

    def o_store(z):
        place = out_ref.at[pl.ds(pl.multiple_of(z * part, part), part), :]
        return pltpu.make_async_copy(chipsum.at[z, chip], place, stored.at[z])

    def held(z):
        return (z != q) & jnp.logical_not(at_end) & ((z == 0) | (z == n_col - 1))

    def finish(z):
        for k in range(1, n_chip):
            r_copy(z, k).wait_recv()
        total = chipsum[z, chip]
        for k in range(1, n_chip):
            total += others[z, k - 1].astype(F32)

        @pl.when(z == q)
        def _():
            chipsum[z, chip] = total
            o_store(z).start()

        @pl.when(z != q)
        def _():
            others[z, 0] = total.astype(others.dtype)

        @pl.when((z != q) & jnp.logical_not(held(z)))
        def _():
            o_copy(z).start()

    @pl.loop(0, n_col)
    def _(i):
        z = order(i)

        @pl.when(i > 0)
        def _():
            line_forward(*d_line, z)
            x_copy(order(i - 1)).wait_send()

        tile = tile_of(d_cols, 256)

        @pl.loop(0, d_cols // tile)
        def _(j):
            cols = pl.ds(pl.multiple_of(j * tile, tile), tile)
            product = jnp.dot(turned[...], dbuf[z, :, cols], preferred_element_type=F32)
            for owner in range(n_row):
                mine[owner % 2, owner // 2, :, cols] = product[owner * part : (owner + 1) * part]

        x_copy(z).start()

        @pl.when(i > 0)
        def _():
            finish(order(i - 1))

        x_copy(z).wait_recv()
        for k in range(1, n_chip):
            target = lax.rem(chip + k, n_chip)
            sent[z, k - 1] = (chipsum[z, target] + mine[core, target]).astype(sent.dtype)
            r_copy(z, k).start()
        chipsum[z, chip] += mine[core, chip]

    last = order(jnp.int32(n_col - 1))
    finish(last)

    x_copy(last).wait_send()
    line_drain(*d_line)

    @pl.loop(0, n_col)
    def _(z):
        @pl.when(held(z))
        def _():
            o_copy(z).start()

    line_drain(*a_line)
    for k in range(1, n_chip):
        b_copy(k).wait_send()
    for k in range(n_chip):
        s_copy(k).wait_send()

    @pl.loop(0, n_col)
    def _(z):
        for k in range(1, n_chip):
            r_copy(z, k).wait_send()

    @pl.loop(1, n_col)
    def _(i):
        z = order(i)
        o_arrival(z).wait_recv()
        chipsum[z, chip] = landed[z].astype(F32)
        o_store(z).start()

    @pl.loop(0, n_col)
    def _(z):
        o_store(z).wait()

        @pl.when(z != q)
        def _():
            o_copy(z).wait_send()

    first_out.wait()


def per_device(n_row, n_col, amplitudes, integrals, dressing):
    rows, depth = amplitudes.shape
    width, d_cols = integrals.shape[1], dressing.shape[1]
    part, n_chip = width // n_row, n_row // 2
    bf16 = amplitudes.dtype
    dma = pltpu.SemaphoreType.DMA
    anywhere = pl.BlockSpec(memory_space=pl.ANY)
    total = depth * n_col
    return tuple(
        pl.pallas_call(
            functools.partial(kernel, n_row, n_col, part),
            out_shape=[
                jax.ShapeDtypeStruct((rows, width), F32),
                jax.ShapeDtypeStruct((part * n_col, d_cols), F32),
            ],
            in_specs=[anywhere] * 3,
            out_specs=[anywhere] * 2,
            scratch_shapes=[
                pltpu.VMEM((n_col, rows, depth), bf16),
                pltpu.VMEM((total, width), bf16),
                pltpu.VMEM((n_col, rows, d_cols), bf16),
                pltpu.VMEM((rows, width), F32),
                pltpu.VMEM((width, rows), bf16),
                pltpu.VMEM((2, n_chip, part, d_cols), F32),
                pltpu.VMEM((n_col, n_chip, part, d_cols), F32),
                pltpu.VMEM((n_col, n_chip - 1, part, d_cols), bf16),
                pltpu.VMEM((n_col, n_chip - 1, part, d_cols), bf16),
                pltpu.VMEM((n_col, part, d_cols), bf16),
                dma((n_col, 2)), dma((n_col,)), dma((n_col, 2)), dma((n_col,)),
                dma((n_chip,)), dma((n_chip,)), dma((n_chip,)), dma((n_chip,)),
                dma((n_col,)), dma((n_col,)),
                dma((n_col, n_chip)), dma((n_col, n_chip)),
                dma((n_col,)), dma((n_col,)), dma((n_col,)),
                dma((4,)),
            ],
            compiler_params=pltpu.CompilerParams(
                collective_id=0, has_side_effects=True, vmem_limit_bytes=62 * 2**20
            ),
            cost_estimate=pl.CostEstimate(
                flops=2 * rows * width * (total + d_cols * n_col),
                bytes_accessed=2 * total * (rows + width),
                transcendentals=0,
            ),
        )(amplitudes, integrals, dressing)
    )


def solution(mesh):
    placed = (P("row", "col"), P("row", "col"), P(None, "col"))
    return jax.shard_map(
        functools.partial(per_device, mesh.shape["row"], mesh.shape["col"]),
        mesh=mesh,
        in_specs=placed,
        out_specs=(P("row", "col"), P("row", "col")),
        check_vma=False,
    )
```

```python
import functools

import jax
import jax.numpy as jnp
from jax import lax
from jax.experimental import pallas as pl
from jax.experimental.pallas import tpu as pltpu
from jax.sharding import PartitionSpec as P

MESH = pl.DeviceIdType.MESH
F32 = jnp.float32


def tile_of(size, largest):
    return max(t for t in range(128, largest + 1, 128) if size % t == 0)


def kernel(
    n_row, n_col, part,
    a_ref, b_ref, d_ref, c_ref, out_ref,
    abuf, bbuf, dbuf, acc, turned, mine, chipsum, sent, others, landed,
    a_send, a_recv, d_send, d_recv, b_send, b_recv, s_send, s_recv,
    x_send, x_recv, r_send, r_recv, o_send, o_recv, stored, loaded_a, loaded_d, loaded_b,
):
    n_chip = n_row // 2
    r, q = lax.axis_index("row"), lax.axis_index("col")
    core, chip = lax.rem(r, 2), lax.div(r, 2)
    sibling = r + 1 - 2 * core
    a_rows, depth = a_ref.shape
    b_rows, width = b_ref.shape
    d_cols = dbuf.shape[2]
    a_cut, d_cut = abuf.shape[0] // n_col, dbuf.shape[0] // n_col
    piece = abuf.shape[2]

    def peer(dist):
        return lax.rem(chip + dist, n_chip) * 2 + core

    def order(i):
        room = jnp.minimum(q, n_col - 1 - q)
        half = lax.div(i + 1, 2)
        near = jnp.where(lax.rem(i, 2) == 1, q - half, q + half)
        far = jnp.where(q <= n_col - 1 - q, i, n_col - 1 - i)
        return jnp.where(i <= 2 * room, near, far)

    def remote(src, dst, send, recv, where):
        return pltpu.make_async_remote_copy(
            src_ref=src, dst_ref=dst, send_sem=send, recv_sem=recv, device_id=where, device_id_type=MESH
        )

    barrier = pltpu.get_barrier_semaphore()
    partners = [{"row": peer(k)} for k in range(1, n_chip)] + [{"row": sibling}]
    partners += [{"col": lax.rem(q + k, n_col)} for k in range(1, n_col)]
    for where in partners:
        pl.semaphore_signal(barrier, inc=1, device_id=where, device_id_type=MESH)
    pl.semaphore_wait(barrier, len(partners))

    def b_slot(owner):
        return bbuf.at[pl.ds(pl.multiple_of(owner * b_rows, b_rows), b_rows), :]

    def b_copy(k):
        return remote(b_ref, b_slot(r), b_send.at[k], b_recv.at[k], {"row": peer(k)})

    def b_arrival(k):
        slot = b_slot(peer(n_chip - k))
        return remote(slot, slot, b_send.at[k], b_recv.at[k], {"row": peer(k)})

    def s_copy(k):
        slot = b_slot(peer(n_chip - k))
        src = b_ref if k == 0 else slot
        return remote(src, slot, s_send.at[k], s_recv.at[k], {"row": sibling})

    def s_arrival(k):
        slot = b_slot(lax.rem(chip + n_chip - k, n_chip) * 2 + 1 - core)
        return remote(slot, slot, s_send.at[k], s_recv.at[k], {"row": sibling})

    def own_a(h):
        return a_ref.at[:, pl.ds(h * piece, piece)]

    def own_d(h):
        rows = pl.ds(pl.multiple_of(r * a_rows, a_rows), a_rows)
        return d_ref.at[rows, pl.ds(h * d_cols, d_cols)]

    def line_copy(buf, send, recv, cut, slot, side, src=None):
        src = buf.at[slot] if src is None else src
        return remote(src, buf.at[slot], send.at[slot, side], recv.at[slot], {"col": q - 1 + 2 * side})

    def line_start(own, buf, send, recv, cut):
        for h in range(cut):

            @pl.when(q > 0)
            def _():
                line_copy(buf, send, recv, cut, q * cut + h, 0, own(h)).start()

            @pl.when(q < n_col - 1)
            def _():
                line_copy(buf, send, recv, cut, q * cut + h, 1, own(h)).start()

    def line_forward(own, buf, send, recv, cut, z, h):
        slot = z * cut + h
        line_copy(buf, send, recv, cut, slot, jnp.where(z < q, 0, 1)).wait_recv()

        @pl.when((z < q) & (q < n_col - 1))
        def _():
            line_copy(buf, send, recv, cut, slot, 1).start()

        @pl.when((z > q) & (q > 0))
        def _():
            line_copy(buf, send, recv, cut, slot, 0).start()

    def line_drain(own, buf, send, recv, cut):
        @pl.loop(0, n_col)
        def _(z):
            for h in range(cut):

                @pl.when((z <= q) & (q < n_col - 1))
                def _():
                    line_copy(buf, send, recv, cut, z * cut + h, 1).wait_send()

                @pl.when((z >= q) & (q > 0))
                def _():
                    line_copy(buf, send, recv, cut, z * cut + h, 0).wait_send()

    a_line = (own_a, abuf, a_send, a_recv, a_cut)
    d_line = (own_d, dbuf, d_send, d_recv, d_cut)

    line_start(*a_line)
    for k in range(1, n_chip):
        b_copy(k).start()
    s_copy(0).start()
    loads = [pltpu.make_async_copy(b_ref, b_slot(r), loaded_b.at[0])]
    for h in range(a_cut):
        loads.append(pltpu.make_async_copy(own_a(h), abuf.at[q * a_cut + h], loaded_a.at[h]))
    for h in range(d_cut):
        loads.append(pltpu.make_async_copy(own_d(h), dbuf.at[q * d_cut + h], loaded_d.at[h]))
    for load in loads:
        load.start()
    for load in loads:
        load.wait()

    at_end = (q == 0) | (q == n_col - 1)
    early = jnp.where(at_end, n_col // 2 + 1, n_col)

    @pl.loop(1, early)
    def _(away):
        for h in range(a_cut):
            for z in (q - away, q + away):

                @pl.when((z >= 0) & (z < n_col))
                def _():
                    line_forward(*a_line, z, h)

    @pl.when(at_end)
    def _():
        line_start(*d_line)

    for k in range(1, n_chip):
        b_arrival(k).wait_recv()
        s_copy(k).start()

    def multiply(slot):
        tile = tile_of(width, 256)

        @pl.loop(0, width // tile)
        def _(j):
            cols = pl.ds(pl.multiple_of(j * tile, tile), tile)
            rows = pl.ds(pl.multiple_of(slot * piece, piece), piece)
            acc[:, cols] += jnp.dot(abuf[slot], bbuf[rows, cols], preferred_element_type=F32)

    acc[...] = jnp.zeros_like(acc)
    for k in range(n_chip):
        s_arrival(k).wait_recv()

    @pl.loop(0, n_col)
    def _(i):
        for h in range(a_cut):

            @pl.when(i >= early)
            def _():
                line_forward(*a_line, order(i), h)

            multiply(order(i) * a_cut + h)

    @pl.when(jnp.logical_not(at_end))
    def _():
        line_start(*d_line)

    first_out = pltpu.make_async_copy(acc, c_ref, loaded_b.at[1])
    first_out.start()
    turn = tile_of(width, 256)

    @pl.loop(0, width // turn)
    def _(j):
        at = pl.ds(pl.multiple_of(j * turn, turn), turn)
        turned[at, :] = acc[:, at].T.astype(turned.dtype)

    def x_copy(z):
        return remote(mine.at[1 - core], chipsum.at[z], x_send.at[z], x_recv.at[z], {"row": sibling})

    def r_copy(z, k):
        return remote(
            sent.at[z, k - 1], others.at[z, k - 1], r_send.at[z, k], r_recv.at[z, k], {"row": peer(k)}
        )

    def line_of(slot):
        return lax.div(slot, d_cut)

    def half_of(slot):
        return lax.rem(slot, d_cut)

    def slot_at(i):
        return order(lax.div(i, d_cut)) * d_cut + lax.rem(i, d_cut)

    def o_copy(slot):
        mark = q * d_cut + half_of(slot)
        return remote(others.at[slot, 0], landed.at[mark], o_send.at[slot], o_recv.at[mark], {"col": line_of(slot)})

    def o_arrival(slot):
        return remote(landed.at[slot], landed.at[slot], o_send.at[slot], o_recv.at[slot], {"col": line_of(slot)})

    def o_store(slot):
        rows = pl.ds(pl.multiple_of(line_of(slot) * part, part), part)
        cols = pl.ds(pl.multiple_of(half_of(slot) * d_cols, d_cols), d_cols)
        return pltpu.make_async_copy(chipsum.at[slot, chip], out_ref.at[rows, cols], stored.at[slot])

    def elsewhere(slot):
        return line_of(slot) != q

    def held(slot):
        z = line_of(slot)
        return (z != q) & jnp.logical_not(at_end) & ((z == 0) | (z == n_col - 1))

    def finish(z):
        for k in range(1, n_chip):
            r_copy(z, k).wait_recv()
        total = chipsum[z, chip]
        for k in range(1, n_chip):
            total += others[z, k - 1].astype(F32)

        @pl.when(jnp.logical_not(elsewhere(z)))
        def _():
            chipsum[z, chip] = total
            o_store(z).start()

        @pl.when(elsewhere(z))
        def _():
            others[z, 0] = total.astype(others.dtype)

        @pl.when(elsewhere(z) & jnp.logical_not(held(z)))
        def _():
            o_copy(z).start()

    @pl.loop(0, n_col * d_cut)
    def _(i):
        z = slot_at(i)

        @pl.when(i >= d_cut)
        def _():
            line_forward(*d_line, line_of(z), half_of(z))

        @pl.when(i > 0)
        def _():
            x_copy(slot_at(i - 1)).wait_send()

        tile = tile_of(d_cols, 384)

        @pl.loop(0, d_cols // tile)
        def _(j):
            cols = pl.ds(pl.multiple_of(j * tile, tile), tile)
            product = jnp.dot(turned[...], dbuf[z, :, cols], preferred_element_type=F32)
            for owner in range(n_row):
                mine[owner % 2, owner // 2, :, cols] = product[owner * part : (owner + 1) * part]

        x_copy(z).start()

        @pl.when(i > 0)
        def _():
            finish(slot_at(i - 1))

        x_copy(z).wait_recv()
        for k in range(1, n_chip):
            target = lax.rem(chip + k, n_chip)
            sent[z, k - 1] = (chipsum[z, target] + mine[core, target]).astype(sent.dtype)
            r_copy(z, k).start()
        chipsum[z, chip] += mine[core, chip]

    last = slot_at(jnp.int32(n_col * d_cut - 1))
    finish(last)

    x_copy(last).wait_send()
    line_drain(*d_line)

    @pl.loop(0, n_col * d_cut)
    def _(z):
        @pl.when(held(z))
        def _():
            o_copy(z).start()

    line_drain(*a_line)
    for k in range(1, n_chip):
        b_copy(k).wait_send()
    for k in range(n_chip):
        s_copy(k).wait_send()

    @pl.loop(0, n_col * d_cut)
    def _(z):
        for k in range(1, n_chip):
            r_copy(z, k).wait_send()

    @pl.loop(d_cut, n_col * d_cut)
    def _(i):
        z = slot_at(i)
        o_arrival(z).wait_recv()
        chipsum[z, chip] = landed[z].astype(F32)
        o_store(z).start()

    @pl.loop(0, n_col * d_cut)
    def _(z):
        o_store(z).wait()

        @pl.when(elsewhere(z))
        def _():
            o_copy(z).wait_send()

    first_out.wait()


def per_device(n_row, n_col, amplitudes, integrals, dressing):
    rows, depth = amplitudes.shape
    width, d_cols = integrals.shape[1], dressing.shape[1]
    part, n_chip = width // n_row, n_row // 2
    bf16 = amplitudes.dtype
    dma = pltpu.SemaphoreType.DMA
    anywhere = pl.BlockSpec(memory_space=pl.ANY)
    total = depth * n_col
    a_cut = 2 if depth % 256 == 0 else 1
    d_cut = 2 if d_cols % 256 == 0 else 1
    d_piece, d_slots = d_cols // d_cut, n_col * d_cut
    return tuple(
        pl.pallas_call(
            functools.partial(kernel, n_row, n_col, part),
            out_shape=[
                jax.ShapeDtypeStruct((rows, width), F32),
                jax.ShapeDtypeStruct((part * n_col, d_cols), F32),
            ],
            in_specs=[anywhere] * 3,
            out_specs=[anywhere] * 2,
            scratch_shapes=[
                pltpu.VMEM((n_col * a_cut, rows, depth // a_cut), bf16),
                pltpu.VMEM((total, width), bf16),
                pltpu.VMEM((d_slots, rows, d_piece), bf16),
                pltpu.VMEM((rows, width), F32),
                pltpu.VMEM((width, rows), bf16),
                pltpu.VMEM((2, n_chip, part, d_piece), F32),
                pltpu.VMEM((d_slots, n_chip, part, d_piece), F32),
                pltpu.VMEM((d_slots, n_chip - 1, part, d_piece), bf16),
                pltpu.VMEM((d_slots, n_chip - 1, part, d_piece), bf16),
                pltpu.VMEM((d_slots, part, d_piece), bf16),
                dma((n_col * a_cut, 2)), dma((n_col * a_cut,)), dma((d_slots, 2)), dma((d_slots,)),
                dma((n_chip,)), dma((n_chip,)), dma((n_chip,)), dma((n_chip,)),
                dma((d_slots,)), dma((d_slots,)),
                dma((d_slots, n_chip)), dma((d_slots, n_chip)),
                dma((d_slots,)), dma((d_slots,)), dma((d_slots,)),
                dma((a_cut,)), dma((d_cut,)), dma((2,)),
            ],
            compiler_params=pltpu.CompilerParams(
                collective_id=0, has_side_effects=True, vmem_limit_bytes=62 * 2**20
            ),
            cost_estimate=pl.CostEstimate(
                flops=2 * rows * width * (total + d_cols * n_col),
                bytes_accessed=2 * total * (rows + width),
                transcendentals=0,
            ),
        )(amplitudes, integrals, dressing)
    )


def solution(mesh):
    placed = (P("row", "col"), P("row", "col"), P(None, "col"))
    return jax.shard_map(
        functools.partial(per_device, mesh.shape["row"], mesh.shape["col"]),
        mesh=mesh,
        in_specs=placed,
        out_specs=(P("row", "col"), P("row", "col")),
        check_vma=False,
    )
```
